256 devices in a mesh: patch: 32 (over z, x_lo, core), tensor: 8 (over y, x_hi).
Axes of the slice: x: 4 (x_hi: 2, x_lo: 2; x = x_hi * 2 + x_lo), y: 4, z: 8, core: 2. Of those that a mesh axis runs over, the one named last changes fastest.
Arguments:
- hidden_in: bfloat16 [12288, 3072], P('patch', 'tensor'), may hold values from -6 to 6
- stale_kv: bfloat16 [2, 12288, 3072], P(None, 'patch', 'tensor'), may hold values from -6 to 6
- mod_table: float32 [28, 3, 3072], replicated, may hold values from -4 to 4
- step_index: int32 [1], replicated, may hold values from 0 to 27
- qkv_weight: bfloat16 [3072, 3, 3072], P(None, None, 'tensor'), may hold values from -0.109375 to 0.109375
- q_gain: float32 [128], replicated, may hold values from 0.5 to 2
- k_gain: float32 [128], replicated, may hold values from 0.5 to 2
- out_weight: bfloat16 [3072, 3072], P('tensor'), may hold values from -0.109375 to 0.109375
Outputs:
- hidden_out: bfloat16 [12288, 3072], P('patch', 'tensor')
- fresh_kv: bfloat16 [2, 12288, 3072], P(None, 'patch', 'tensor')
The draws below stay inside these ranges and needn't reach their ends.
All inputs are finite; a program needn't handle non-finite values.
Results may differ from the reference program's by a relative error of at most 0.008.
Values may be sent and summed in bfloat16 or wider, within the bound.
No kernel may reach another device: no remote copies, remote signals or barrier semaphores. Data moves between devices by JAX's collectives and lax.ppermute only.
A program may use at most 192 MiB of HBM per device.

```python
import math
import jax
import jax.numpy as jnp
from jax import lax

HEADS = 24
HEAD = 128
D = 3072
STEPS = 28
TOK_DEV = 384
TOKENS = 12288
N_PATCH = 32


def level_of(own_key, extent, pieces, least, high):
    level = 1.0
    for dim, shards_of in pieces:
        draws = jax.random.uniform(jax.random.fold_in(jax.random.fold_in(own_key, 6), dim), (shards_of,), jnp.float32, least / len(pieces), high / len(pieces))
        level = level * jnp.repeat(jnp.exp(draws), extent[dim] // shards_of).reshape((-1,) + (1,) * (len(extent) - 1 - dim))
    return level


def gaussian(own_key, shape, deviation, reach, pieces=(), held_as=jnp.bfloat16):
    drawn = deviation * jax.random.normal(own_key, shape, jnp.float32)
    if pieces:
        drawn = drawn * level_of(own_key, shape, pieces, -0.22, 0.18)
    return jnp.clip(drawn, -reach, reach).astype(held_as)


def setup_inputs(seed: int = 0) -> dict:
    arg_keys = jax.random.split(jax.random.key(seed), 9)
    hidden_in = gaussian(arg_keys[0], (TOKENS, D), 1.0, 6.0, ((0, 32), (1, 8)))
    stale_kv = gaussian(arg_keys[1], (2, TOKENS, D), 1.0, 6.0, ((1, 32), (2, 8)))
    mod_table = gaussian(arg_keys[2], (STEPS, 3, D), 1.0, 4.0, (), jnp.float32)
    step_index = jax.random.randint(arg_keys[3], (1,), 0, STEPS).astype(jnp.int32)
    qkv_weight = gaussian(arg_keys[4], (D, 3, D), D ** -0.5, 0.109375, ((2, 8),))
    q_gain = jnp.clip(jnp.exp(jax.random.uniform(arg_keys[5], (HEAD,), jnp.float32, math.log(0.5), math.log(2.0))), 0.5, 2.0)
    k_gain = jnp.clip(jnp.exp(jax.random.uniform(arg_keys[6], (HEAD,), jnp.float32, math.log(0.5), math.log(2.0))), 0.5, 2.0)
    out_weight = gaussian(arg_keys[7], (D, D), D ** -0.5, 0.109375, ((0, 8),))
    return dict(hidden_in=hidden_in, stale_kv=stale_kv, mod_table=mod_table, step_index=step_index, qkv_weight=qkv_weight, q_gain=q_gain, k_gain=k_gain, out_weight=out_weight)


def head_norm(u, gain):
    return u * lax.rsqrt(lax.optimization_barrier(jnp.mean(u * u, axis=-1, keepdims=True)) + 1e-06) * gain

def reference(hidden_in, stale_kv, mod_table, step_index, qkv_weight, q_gain, k_gain, out_weight):
    modulation = lax.dynamic_index_in_dim(mod_table, step_index[0].astype(jnp.int32), 0, keepdims=False)
    shift, scale, gate = (modulation[0], modulation[1], modulation[2])
    x = hidden_in.astype(jnp.float32)
    mean = lax.optimization_barrier(jnp.mean(x, axis=-1, keepdims=True))
    var = lax.optimization_barrier(jnp.mean((x - mean) ** 2, axis=-1, keepdims=True))
    normed = ((x - mean) * lax.rsqrt(var + 1e-06) * (1.0 + scale) + shift).astype(jnp.bfloat16)
    qkv = jnp.dot(normed, qkv_weight.reshape(D, 3 * D), preferred_element_type=jnp.float32)
    qkv = qkv.reshape(TOKENS, 3, HEADS, HEAD)
    query = head_norm(qkv[:, 0], q_gain).astype(jnp.bfloat16)
    key_new = head_norm(qkv[:, 1], k_gain).astype(jnp.bfloat16)
    value_new = qkv[:, 2].astype(jnp.bfloat16)
    fresh_kv = jnp.stack([key_new.reshape(TOKENS, D), value_new.reshape(TOKENS, D)])
    factor = HEAD ** (-0.5)

    def one_patch(index):
        start = (index * TOK_DEV).astype(jnp.int32)
        q_block = lax.dynamic_slice_in_dim(query, start, TOK_DEV, 0).astype(jnp.float32)
        own = lax.dynamic_slice_in_dim(fresh_kv, start, TOK_DEV, 1)
        merged = lax.dynamic_update_slice_in_dim(stale_kv, own, start, 1)
        keys = merged[0].reshape(TOKENS, HEADS, HEAD).astype(jnp.float32)
        values = merged[1].reshape(TOKENS, HEADS, HEAD).astype(jnp.float32)
        scores = jnp.einsum('thd,shd->hts', q_block, keys) * factor
        top = lax.optimization_barrier(jnp.max(scores, axis=-1, keepdims=True))
        expo = jnp.exp(scores - top)
        total = lax.optimization_barrier(jnp.sum(expo, axis=-1))
        weights = lax.optimization_barrier(expo.astype(jnp.bfloat16)).astype(jnp.float32)
        acc = jnp.einsum('hts,shd->htd', weights, values)
        out = acc / total[..., None]
        return jnp.transpose(out, (1, 0, 2)).reshape(TOK_DEV, D).astype(jnp.bfloat16)
    attn = lax.map(one_patch, jnp.arange(N_PATCH, dtype=jnp.int32)).reshape(TOKENS, D)
    proj = jnp.dot(attn, out_weight, preferred_element_type=jnp.float32)
    hidden_out = (x + gate * proj).astype(jnp.bfloat16)
    return (hidden_out, fresh_kv)
```

```python
import jax
import jax.numpy as jnp
from jax import lax
from jax.experimental import pallas as pl
from jax.experimental.pallas import tpu as pltpu
from jax.sharding import PartitionSpec as P

HEAD = 128
D = 3072
W = 384
HL = 3
TOK = 384
NZ, NY = 8, 4
LOG2E = 1.4426950408889634
F32, BF16 = jnp.float32, jnp.bfloat16
VMEM = pl.BlockSpec(memory_space=pltpu.VMEM)
SMEM = pl.BlockSpec(memory_space=pltpu.SMEM)
ANY = pl.BlockSpec(memory_space=pl.ANY)
HBM = pl.BlockSpec(memory_space=pltpu.HBM)


def move(x, axis, dz=0, dxl=0, dc=0, dy=0, dxh=0):
    if axis == "patch":
        pairs = [
            (i, ((i // 4 + dz) % NZ) * 4 + (((i // 2) % 2) ^ dxl) * 2 + ((i % 2) ^ dc))
            for i in range(32)
        ]
    else:
        pairs = [(i, ((i // 2 + dy) % NY) * 2 + ((i % 2) ^ dxh)) for i in range(8)]
    return lax.ppermute(x, axis, pairs)


def call(kern, outs, n_in, flops, smem=(), hbm=(), late=(), scratch=(), name=None, mb=32):
    return pl.pallas_call(
        kern,
        out_shape=tuple(jax.ShapeDtypeStruct(s, t) for s, t in outs),
        in_specs=[
            SMEM if i in smem else HBM if i in hbm else ANY if i in late else VMEM
            for i in range(n_in)
        ],
        out_specs=tuple(VMEM for _ in outs),
        scratch_shapes=list(scratch),
        compiler_params=pltpu.CompilerParams(vmem_limit_bytes=mb * 2**20),
        cost_estimate=pl.CostEstimate(flops=flops, bytes_accessed=4 * 2**20, transcendentals=0),
        name=name,
    )


def qkv_kernel(rank_ref, *refs):
    a = refs[0:4]
    b = refs[4:8]
    bx = refs[8]
    mod_ref, gain_ref, w_hbm, q_ref, f_ref, n_ref, w_ref, sem = refs[9:]
    half = TOK // 2
    copies = [
        pltpu.make_async_copy(w_hbm.at[j], w_ref.at[:, j * W : j * W + W], sem.at[j])
        for j in range(3)
    ]
    for cp in copies:
        cp.start()

    def pieces(r):
        for dy in range(NY):
            for dx in range(2):
                if r == 0:
                    x = a[dy][:, dx * W : dx * W + W]
                else:
                    x = b[dy][...] if dx == 0 else bx[:, dy * W : dy * W + W]
                yield dy * 2 + dx, x.astype(F32)

    for r in range(2):
        total = None
        for _, x in pieces(r):
            total = x if total is None else total + x
        mean = jnp.sum(total, axis=1, keepdims=True) * (1.0 / D)
        total = None
        for _, x in pieces(r):
            c = x - mean
            total = c * c if total is None else total + c * c
        rstd = lax.rsqrt(jnp.sum(total, axis=1, keepdims=True) * (1.0 / D) + 1e-06)
        for j, x in pieces(r):
            cols = pl.ds(pl.multiple_of(rank_ref[j] * W, W), W)
            shift = mod_ref[0:1, cols]
            scale = mod_ref[1:2, cols]
            n_ref[r * half : r * half + half, cols] = (
                (x - mean) * rstd * (1.0 + scale) + shift
            ).astype(BF16)

    def head_norm(u, gain):
        out = []
        for h in range(HL):
            v = u[:, h * HEAD : h * HEAD + HEAD]
            ms = jnp.mean(v * v, axis=1, keepdims=True)
            out.append(v * lax.rsqrt(ms + 1e-06) * gain)
        return jnp.concatenate(out, axis=1)

    for cp in copies:
        cp.wait()
    qkv = jnp.dot(n_ref[...], w_ref[...], preferred_element_type=F32)
    q_ref[...] = head_norm(qkv[:, :W], gain_ref[0:1, :] * (HEAD**-0.5 * LOG2E)).astype(BF16)
    f_ref[0] = head_norm(qkv[:, W : 2 * W], gain_ref[1:2, :]).astype(BF16)
    f_ref[1] = qkv[:, 2 * W :].astype(BF16)


def flash(hs, q, blocks, m, l, acc):
    groups = [blocks[i : i + 2] for i in range(0, len(blocks), 2)]

    def scores(g):
        k = [kb(hs) for kb, _ in g]
        k = k[0] if len(k) == 1 else jnp.concatenate(k, axis=0)
        return lax.dot_general(q, k, (((1,), (1,)), ((), ())), preferred_element_type=F32)

    s = scores(groups[0])
    for i, g in enumerate(groups):
        nxt = scores(groups[i + 1]) if i + 1 < len(groups) else None
        top = jnp.max(s, axis=1, keepdims=True)
        new = top if m is None else jnp.maximum(m, top)
        p = jnp.exp2(s - new)
        ls = p[:, :HEAD]
        for j in range(1, p.shape[1] // HEAD):
            ls = ls + p[:, j * HEAD : j * HEAD + HEAD]
        ls = jnp.sum(ls, axis=1, keepdims=True)
        v = [vb(hs) for _, vb in g]
        v = v[0] if len(v) == 1 else jnp.concatenate(v, axis=0)
        pv = jnp.dot(p.astype(BF16), v, preferred_element_type=F32)
        if m is None:
            l, acc = ls, pv
        else:
            a = jnp.exp2(m - new)
            l, acc = l * a + ls, acc * a + pv
        m, s = new, nxt
    return m, l, acc


def views(refs, kinds):
    out, i = [], 0
    for kind in kinds:
        if kind == 2:
            r = refs[i]
            out.append((lambda hs, r=r: r[0, :, hs], lambda hs, r=r: r[1, :, hs]))
            i += 1
        else:
            rk, rv = refs[i], refs[i + 1]
            out.append((lambda hs, r=rk: r[:, hs], lambda hs, r=rv: r[:, hs]))
            i += 2
    return out


def head_slice(h):
    return pl.ds(pl.multiple_of(h * HEAD, HEAD), HEAD)


def first_stage(q, blocks, name, after=()):
    rows = q.shape[0]
    kinds = [2] * len(blocks)

    def kern(q_ref, *refs):
        kv = views(refs, kinds)
        acc_ref, m_ref, l_ref = refs[-3:]

        @pl.loop(0, HL)
        def _(h):
            hs = head_slice(h)
            m, l, acc = flash(hs, q_ref[:, hs], kv, None, None, None)
            acc_ref[:, hs] = acc
            m_ref[:, hs] = jnp.broadcast_to(m, (rows, HEAD))
            l_ref[:, hs] = jnp.broadcast_to(l, (rows, HEAD))

    n = 1 + len(blocks)
    return call(
        kern,
        [((rows, W), F32)] * 3,
        n + len(after),
        4 * rows * W * TOK * len(blocks),
        late=range(n, n + len(after)),
        name=name,
    )(q, *blocks, *after)


def second_stage(q, state, refs_in, kinds, chunk, rows, name, after=()):
    def kern(q_ref, acc_ref, m_ref, l_ref, *refs):
        kv = views(refs, kinds)
        o_ref = refs[-1]
        rs = slice(chunk * rows, chunk * rows + rows)
        lane = lax.broadcasted_iota(jnp.int32, (rows, HEAD), 1)
        o_ref[:, W : W + HEAD] = jnp.zeros((rows, HEAD), BF16)

        @pl.loop(0, HL)
        def _(h):
            hs = head_slice(h)
            m, l, acc = flash(
                hs, q_ref[rs, hs], kv, m_ref[rs, hs][:, :1], l_ref[rs, hs][:, :1], acc_ref[rs, hs]
            )
            o_ref[:, hs] = (acc / l).astype(BF16)
            lse = m + jnp.log2(l)
            hi = lse.astype(BF16).astype(F32)
            mid = (lse - hi).astype(BF16).astype(F32)
            low = lse - hi - mid
            row = jnp.where(lane == 3 * h, hi, 0.0)
            row = jnp.where(lane == 3 * h + 1, mid, row)
            row = jnp.where(lane == 3 * h + 2, low, row)
            o_ref[:, W : W + HEAD] = (o_ref[:, W : W + HEAD].astype(F32) + row).astype(BF16)

    n = 4 + len(refs_in)
    return call(
        kern,
        [((rows, W + HEAD), BF16)],
        n + len(after),
        4 * rows * W * TOK * len(kinds),
        late=range(n, n + len(after)),
        name=name,
    )(q, *state, *refs_in, *after)[0]


def project(mine, other, w, rank, rows, name):
    def kern(rank_ref, a_ref, b_ref, w_ref, *o_refs):
        la = a_ref[:, W : W + HEAD].astype(F32)
        lb = b_ref[:, W : W + HEAD].astype(F32)
        out = []
        for h in range(HL):
            x = jnp.sum(la[:, 3 * h : 3 * h + 3], axis=1, keepdims=True)
            y = jnp.sum(lb[:, 3 * h : 3 * h + 3], axis=1, keepdims=True)
            top = jnp.maximum(x, y)
            x, y = jnp.exp2(x - top), jnp.exp2(y - top)
            inv = 1.0 / (x + y)
            s = slice(h * HEAD, h * HEAD + HEAD)
            out.append(
                a_ref[:, s].astype(F32) * (x * inv) + b_ref[:, s].astype(F32) * (y * inv)
            )
        attn = jnp.concatenate(out, axis=1).astype(BF16)
        for j in range(8):
            cols = pl.ds(pl.multiple_of(rank_ref[j] * W, W), W)
            o_refs[j][...] = jnp.dot(
                attn, w_ref[:, cols], preferred_element_type=F32
            ).astype(BF16)

    def whole(rank_ref, a_ref, b_ref, w_ref, *o_refs):
        parts = []
        for o in o_refs:
            for j in range(o.shape[1] // W):
                parts.append(o.at[:, j * W : j * W + W])
        order = sorted(range(8), key=lambda i: layout[i])
        refs = [None] * 8
        for i, r in zip(layout, parts):
            refs[i] = r
        kern(rank_ref, a_ref, b_ref, w_ref, *refs)

    if name.endswith("a"):
        layout = [dy * 2 + dx for dy in range(NY) for dx in range(2)]
        outs = [((rows, 2 * W), BF16)] * 4
    else:
        layout = [dy * 2 + dx for dx in range(2) for dy in range(NY)]
        outs = [((rows, 4 * W), BF16)] * 2
    return call(whole, outs, 4, 2 * rows * W * D, smem=(0,), name=name)(rank, mine, other, w)


def on_device(hidden_in, stale_kv, mod_table, step_index, qkv_weight, q_gain, k_gain, out_weight):
    half = TOK // 2
    t_idx = lax.axis_index("tensor")
    y_idx, x_idx = t_idx // 2, t_idx % 2
    rank = jnp.stack(
        [((y_idx + dy) % NY) * 2 + (x_idx ^ dx) for dy in range(NY) for dx in range(2)]
    ).astype(jnp.int32)
    modulation = lax.dynamic_index_in_dim(mod_table, step_index[0], 0, keepdims=False)
    gate = lax.dynamic_slice_in_dim(modulation[2], t_idx * W, W, 0)
    gains = jnp.stack([q_gain, k_gain])
    weight = jnp.transpose(qkv_weight, (1, 0, 2))
    tie = lax.optimization_barrier

    ha, hb = hidden_in[:half], hidden_in[half:]
    pa = jnp.concatenate([ha, move(ha, "tensor", dxh=1)], axis=1)
    gb = {0: hb, 1: move(hb, "tensor", dy=-1), 3: move(hb, "tensor", dy=1)}
    hb2, gb[1] = tie((hb, gb[1]))
    gb[2] = move(hb2, "tensor", dy=2)
    ga = {0: pa, 1: move(pa, "tensor", dy=-1), 3: move(pa, "tensor", dy=1)}
    pa2, gb[2] = tie((pa, gb[2]))
    ga[2] = move(pa2, "tensor", dy=2)
    gbx = move(jnp.concatenate([gb[d] for d in range(NY)], axis=1), "tensor", dxh=1)

    tokens = []

    def after(xs, deps):
        out = tie((*xs, *deps))
        tokens.extend(out[len(xs) :])
        return out[: len(xs)]

    x0 = stale_kv
    up, down = [x0], [x0]
    gates = [(), (gb[1], pa), (ga[1], ga[3])]
    for deps in gates:
        u, d = after((up[-1], down[-1]), deps) if deps else (x0, x0)
        up.append(move(u, "patch", dz=1))
        down.append(move(d, "patch", dz=-1))
    u, d = after((up[3], down[3]), (gbx, ga[2]))
    k4 = move(u[0], "patch", dz=1)
    v4 = move(d[1], "patch", dz=-1)

    def swap(x):
        return move(x, "patch", dc=1)

    near = [x0, up[1], down[1], up[2], down[2]]
    near_c = [swap(x) for x in after(near, (gbx, ga[2]))]

    q, fresh = call(
        qkv_kernel,
        [((TOK, W), BF16), ((2, TOK, W), BF16)],
        13,
        2 * TOK * D * 3 * W,
        smem=(0,),
        hbm=(12,),
        scratch=[
            pltpu.VMEM((TOK, D), BF16),
            pltpu.VMEM((D, 3 * W), BF16),
            pltpu.SemaphoreType.DMA((3,)),
        ],
        name="qkv",
    )(
        rank,
        *[ga[d] for d in range(NY)],
        *[gb[d] for d in range(NY)],
        gbx,
        modulation,
        gains,
        weight,
    )
    q_other = move(q, "patch", dxl=1)
    own1 = first_stage(q, [*near[1:], *near_c], "own_first", after=tokens)
    par1 = first_stage(q_other, [*near, *near_c], "partner_first", after=own1[:1])
    far = [up[3], down[3], k4, v4]
    far_c = [swap(x) for x in far]
    rest = [*far, *far_c]
    kinds = [2, 2, 1] * 2
    sent = []
    for c in range(2):
        sent.append(
            second_stage(
                q_other, par1, rest, kinds, c, half, f"partner_second_{c}", after=sent[-1:]
            )
        )
    got = [move(x, "patch", dxl=1) for x in sent]
    mine = second_stage(
        q, own1, [fresh, *rest], [2, *kinds], 0, half, "own_second_0", after=sent[-1:]
    )
    outs_a = project(mine, got[0], out_weight, rank, half, "project_a")
    mine = second_stage(
        q, own1, [fresh, *rest], [2, *kinds], 1, half, "own_second_1", after=outs_a[:1]
    )
    outs_b = project(mine, got[1], out_weight, rank, half, "project_b")
    acc = outs_a[0].astype(F32)
    for dy in range(1, NY):
        acc = acc + move(outs_a[dy], "tensor", dy=dy).astype(F32)
    proj_a = acc[:, :W] + move(acc[:, W:].astype(BF16), "tensor", dxh=1).astype(F32)
    acc = outs_b[0].astype(F32) + move(outs_b[1], "tensor", dxh=1).astype(F32)
    proj_b = acc[:, :W]
    for dy in range(1, NY):
        proj_b = proj_b + move(
            acc[:, dy * W : dy * W + W].astype(BF16), "tensor", dy=dy
        ).astype(F32)
    proj = jnp.concatenate([proj_a, proj_b], axis=0)
    hidden_out = (hidden_in.astype(F32) + gate * proj).astype(BF16)
    return hidden_out, fresh


def solution(mesh):
    in_specs = (
        P("patch", "tensor"),
        P(None, "patch", "tensor"),
        P(),
        P(),
        P(None, None, "tensor"),
        P(),
        P(),
        P("tensor", None),
    )
    out_specs = (P("patch", "tensor"), P(None, "patch", "tensor"))
    return jax.shard_map(
        on_device, mesh=mesh, in_specs=in_specs, out_specs=out_specs, check_vma=False
    )
```

```python
import jax
import jax.numpy as jnp
from jax import lax
from jax.experimental import pallas as pl
from jax.experimental.pallas import tpu as pltpu
from jax.sharding import PartitionSpec as P

HEAD = 128
D = 3072
W = 384
HL = 3
TOK = 384
NZ, NY = 8, 4
LOG2E = 1.4426950408889634
F32, BF16 = jnp.float32, jnp.bfloat16
VMEM = pl.BlockSpec(memory_space=pltpu.VMEM)
SMEM = pl.BlockSpec(memory_space=pltpu.SMEM)
ANY = pl.BlockSpec(memory_space=pl.ANY)
HBM = pl.BlockSpec(memory_space=pltpu.HBM)


def move(x, axis, dz=0, dxl=0, dc=0, dy=0, dxh=0):
    if axis == "patch":
        pairs = [
            (i, ((i // 4 + dz) % NZ) * 4 + (((i // 2) % 2) ^ dxl) * 2 + ((i % 2) ^ dc))
            for i in range(32)
        ]
    else:
        pairs = [(i, ((i // 2 + dy) % NY) * 2 + ((i % 2) ^ dxh)) for i in range(8)]
    return lax.ppermute(x, axis, pairs)


def call(kern, outs, n_in, flops, smem=(), hbm=(), late=(), scratch=(), name=None, mb=24):
    return pl.pallas_call(
        kern,
        out_shape=tuple(jax.ShapeDtypeStruct(s, t) for s, t in outs),
        in_specs=[
            SMEM if i in smem else HBM if i in hbm else ANY if i in late else VMEM
            for i in range(n_in)
        ],
        out_specs=tuple(VMEM for _ in outs),
        scratch_shapes=list(scratch),
        compiler_params=pltpu.CompilerParams(vmem_limit_bytes=mb * 2**20),
        cost_estimate=pl.CostEstimate(flops=flops, bytes_accessed=4 * 2**20, transcendentals=0),
        name=name,
    )


def qkv_kernel(g_hbm, mod_ref, gain_ref, w_hbm, q_ref, f_ref, n_ref, w_ref, g_ref, sem):
    gather = pltpu.make_async_copy(g_hbm, g_ref, sem.at[3])
    gather.start()
    copies = [
        pltpu.make_async_copy(w_hbm.at[j], w_ref.at[:, j * W : j * W + W], sem.at[j])
        for j in range(3)
    ]
    for cp in copies:
        cp.start()
    n = D // W
    gather.wait()

    @pl.loop(0, TOK // 64)
    def _(r):
        rows = pl.ds(pl.multiple_of(r * 64, 64), 64)
        x = [g_ref[j, rows, :].astype(F32) for j in range(n)]
        total = x[0]
        for j in range(1, n):
            total = total + x[j]
        mean = jnp.sum(total, axis=1, keepdims=True) * (1.0 / D)
        x = [v - mean for v in x]
        total = x[0] * x[0]
        for j in range(1, n):
            total = total + x[j] * x[j]
        rstd = lax.rsqrt(jnp.sum(total, axis=1, keepdims=True) * (1.0 / D) + 1e-06)
        for j in range(n):
            cols = slice(j * W, j * W + W)
            n_ref[rows, cols] = (
                x[j] * rstd * (1.0 + mod_ref[1:2, cols]) + mod_ref[0:1, cols]
            ).astype(BF16)

    def head_norm(u, gain):
        out = []
        for h in range(HL):
            v = u[:, h * HEAD : h * HEAD + HEAD]
            ms = jnp.mean(v * v, axis=1, keepdims=True)
            out.append(v * lax.rsqrt(ms + 1e-06) * gain)
        return jnp.concatenate(out, axis=1)

    for cp in copies:
        cp.wait()
    qkv = jnp.dot(n_ref[...], w_ref[...], preferred_element_type=F32)
    q_ref[...] = head_norm(qkv[:, :W], gain_ref[0:1, :] * (HEAD**-0.5 * LOG2E)).astype(BF16)
    f_ref[0] = head_norm(qkv[:, W : 2 * W], gain_ref[1:2, :]).astype(BF16)
    f_ref[1] = qkv[:, 2 * W :].astype(BF16)


def flash(hs, q, blocks, m, l, acc):
    groups = [blocks[i : i + 2] for i in range(0, len(blocks), 2)]

    def scores(g):
        k = [kb(hs) for kb, _ in g]
        k = k[0] if len(k) == 1 else jnp.concatenate(k, axis=0)
        return lax.dot_general(q, k, (((1,), (1,)), ((), ())), preferred_element_type=F32)

    s = scores(groups[0])
    for i, g in enumerate(groups):
        nxt = scores(groups[i + 1]) if i + 1 < len(groups) else None
        top = jnp.max(s, axis=1, keepdims=True)
        new = top if m is None else jnp.maximum(m, top)
        p = jnp.exp2(s - new)
        ls = p[:, :HEAD]
        for j in range(1, p.shape[1] // HEAD):
            ls = ls + p[:, j * HEAD : j * HEAD + HEAD]
        ls = jnp.sum(ls, axis=1, keepdims=True)
        v = [vb(hs) for _, vb in g]
        v = v[0] if len(v) == 1 else jnp.concatenate(v, axis=0)
        pv = jnp.dot(p.astype(BF16), v, preferred_element_type=F32)
        if m is None:
            l, acc = ls, pv
        else:
            a = jnp.exp2(m - new)
            l, acc = l * a + ls, acc * a + pv
        m, s = new, nxt
    return m, l, acc


def views(refs, kinds):
    out, i = [], 0
    for kind in kinds:
        if kind == 2:
            r = refs[i]
            out.append((lambda hs, r=r: r[0, :, hs], lambda hs, r=r: r[1, :, hs]))
            i += 1
        else:
            rk, rv = refs[i], refs[i + 1]
            out.append((lambda hs, r=rk: r[:, hs], lambda hs, r=rv: r[:, hs]))
            i += 2
    return out


def head_slice(h):
    return pl.ds(pl.multiple_of(h * HEAD, HEAD), HEAD)


def first_stage(q, blocks, name, after=()):
    rows = q.shape[0]
    kinds = [2] * len(blocks)

    def kern(q_ref, *refs):
        kv = views(refs, kinds)
        acc_ref, ml_ref = refs[-2:]
        lane = lax.broadcasted_iota(jnp.int32, (rows, HEAD), 1)
        ml_ref[...] = jnp.zeros((rows, HEAD), F32)

        @pl.loop(0, HL)
        def _(h):
            hs = head_slice(h)
            m, l, acc = flash(hs, q_ref[:, hs], kv, None, None, None)
            acc_ref[:, hs] = acc
            ml = jnp.where(lane == h, m, ml_ref[...])
            ml_ref[...] = jnp.where(lane == HL + h, l, ml)

    n = 1 + len(blocks)
    return call(
        kern,
        [((rows, W), F32), ((rows, HEAD), F32)],
        n + len(after),
        12 * rows * W * TOK * len(blocks),
        late=range(n, n + len(after)),
        name=name,
    )(q, *blocks, *after)


def second_stage(q, state, refs_in, kinds, first, rows, name, after=(), cost=12):
    def kern(q_ref, acc_ref, ml_ref, *refs):
        kv = views(refs, kinds)
        o_ref = refs[-1]
        rs = slice(first, first + rows)
        lane = lax.broadcasted_iota(jnp.int32, (rows, HEAD), 1)
        o_ref[:, W : W + HEAD] = jnp.zeros((rows, HEAD), BF16)

        @pl.loop(0, HL)
        def _(h):
            hs = head_slice(h)
            ml = ml_ref[rs, :]
            m = jnp.sum(jnp.where(lane == h, ml, 0.0), axis=1, keepdims=True)
            l = jnp.sum(jnp.where(lane == HL + h, ml, 0.0), axis=1, keepdims=True)
            m, l, acc = flash(hs, q_ref[rs, hs], kv, m, l, acc_ref[rs, hs])
            o_ref[:, hs] = (acc / l).astype(BF16)
            lse = m + jnp.log2(l)
            hi = lse.astype(BF16).astype(F32)
            mid = (lse - hi).astype(BF16).astype(F32)
            low = lse - hi - mid
            row = jnp.where(lane == 3 * h, hi, 0.0)
            row = jnp.where(lane == 3 * h + 1, mid, row)
            row = jnp.where(lane == 3 * h + 2, low, row)
            o_ref[:, W : W + HEAD] = (o_ref[:, W : W + HEAD].astype(F32) + row).astype(BF16)

    n = 3 + len(refs_in)
    return call(
        kern,
        [((rows, W + HEAD), BF16)],
        n + len(after),
        cost * rows * W * TOK * len(kinds),
        late=range(n, n + len(after)),
        name=name,
    )(q, *state, *refs_in, *after)[0]


def project(mine, other, w, rank, rows, name, after=()):
    def kern(rank_ref, a_ref, b_ref, w_ref, *o_refs):
        la = a_ref[:, W : W + HEAD].astype(F32)
        lb = b_ref[:, W : W + HEAD].astype(F32)
        out = []
        for h in range(HL):
            x = jnp.sum(la[:, 3 * h : 3 * h + 3], axis=1, keepdims=True)
            y = jnp.sum(lb[:, 3 * h : 3 * h + 3], axis=1, keepdims=True)
            top = jnp.maximum(x, y)
            x, y = jnp.exp2(x - top), jnp.exp2(y - top)
            inv = 1.0 / (x + y)
            s = slice(h * HEAD, h * HEAD + HEAD)
            out.append(
                a_ref[:, s].astype(F32) * (x * inv) + b_ref[:, s].astype(F32) * (y * inv)
            )
        attn = jnp.concatenate(out, axis=1).astype(BF16)
        for j in range(8):
            cols = pl.ds(pl.multiple_of(rank_ref[j] * W, W), W)
            o_refs[j][...] = jnp.dot(
                attn, w_ref[:, cols], preferred_element_type=F32
            ).astype(BF16)

    def whole(rank_ref, a_ref, b_ref, w_ref, *o_refs):
        o_refs = o_refs[len(after) :]
        parts = []
        for o in o_refs:
            for j in range(o.shape[1] // W):
                parts.append(o.at[:, j * W : j * W + W])
        refs = [None] * 8
        for i, r in zip(layout, parts):
            refs[i] = r
        kern(rank_ref, a_ref, b_ref, w_ref, *refs)

    if name.endswith("a"):
        layout = [dy * 2 + dx for dy in range(NY) for dx in range(2)]
        outs = [((rows, 2 * W), BF16)] * 4
    else:
        layout = [dy * 2 + dx for dx in range(2) for dy in range(NY)]
        outs = [((rows, 4 * W), BF16)] * 2
    n = 4 + len(after)
    return call(
        whole, outs, n, 2 * rows * W * D, smem=(0,), late=range(4, n), name=name
    )(rank, mine, other, w, *after)


def on_device(hidden_in, stale_kv, mod_table, step_index, qkv_weight, q_gain, k_gain, out_weight):
    t_idx = lax.axis_index("tensor")
    y_idx, x_idx = t_idx // 2, t_idx % 2
    rank = jnp.stack(
        [((y_idx + dy) % NY) * 2 + (x_idx ^ dx) for dy in range(NY) for dx in range(2)]
    ).astype(jnp.int32)
    modulation = lax.dynamic_index_in_dim(mod_table, step_index[0], 0, keepdims=False)
    gate = lax.dynamic_slice_in_dim(modulation[2], t_idx * W, W, 0)
    gains = jnp.stack([q_gain, k_gain])
    in_hbm = pltpu.with_memory_space_constraint
    weight = in_hbm(jnp.transpose(qkv_weight, (1, 0, 2)), pltpu.HBM)
    tie = lax.optimization_barrier

    hidden = lax.all_to_all(
        jnp.broadcast_to(hidden_in[None], (8, TOK, W)), "tensor", 0, 0, tiled=True
    )

    def step(u, d):
        return move(u, "patch", dz=1), move(d, "patch", dz=-1)

    def swap(*xs):
        return [move(x, "patch", dc=1) for x in xs]

    x0 = stale_kv
    up1, down1 = step(x0, x0)
    up2, down2 = step(up1, down1)
    x0c, up1c, down1c = swap(x0, up1, down1)
    x0c, up1c, down1c, up2, down2 = tie((x0c, up1c, down1c, up2, down2))
    up3, down3 = step(up2, down2)
    up2c, down2c = swap(up2, down2)
    near = [x0, up1, down1, up2, down2]
    near_c = [x0c, up1c, down1c, up2c, down2c]

    q, fresh = call(
        qkv_kernel,
        [((TOK, W), BF16), ((2, TOK, W), BF16)],
        4,
        6 * TOK * D * 3 * W,
        hbm=(0, 3),
        scratch=[
            pltpu.VMEM((TOK, D), BF16),
            pltpu.VMEM((D, 3 * W), BF16),
            pltpu.VMEM((8, TOK, W), BF16),
            pltpu.SemaphoreType.DMA((4,)),
        ],
        name="qkv",
    )(in_hbm(hidden, pltpu.HBM), modulation, gains, weight)
    up3, down3, q = tie((up3, down3, q))
    q_other = move(q, "patch", dxl=1)
    own1 = first_stage(q, [*near[1:], *near_c], "own_first")
    k4, v4 = step(up3[0], down3[1])
    par1 = first_stage(q_other, [*near, *near_c], "partner_first", after=own1[:1])
    far = [up3, down3, k4, v4]
    rest = [*far, *swap(*far)]
    kinds = [2, 2, 1] * 2
    rows_a, rows_b = 256, 128
    fresh_rest, fresh_kinds = [fresh, *rest], [2, *kinds]
    sent_a = second_stage(q_other, par1, rest, kinds, 0, rows_a, "partner_second_a")
    got_a = move(sent_a, "patch", dxl=1)
    mine_a = second_stage(
        q, own1, fresh_rest, fresh_kinds, 0, rows_a, "own_second_a", after=[sent_a]
    )
    outs_a = project(mine_a, got_a, out_weight, rank, rows_a, "project_a")
    near_a = [move(outs_a[dy], "tensor", dy=dy) for dy in (1, 3)]
    sent_b = second_stage(
        q_other, par1, rest, kinds, rows_a, rows_b, "partner_second_b", after=outs_a[:1]
    )
    got_b = move(sent_b, "patch", dxl=1)
    mine_b = second_stage(
        q, own1, fresh_rest, fresh_kinds, rows_a, rows_b, "own_second_b", after=[sent_b]
    )
    outs_b = project(mine_b, got_b, out_weight, rank, rows_b, "project_b")
    acc = outs_a[0].astype(F32) + near_a[0].astype(F32) + near_a[1].astype(F32)
    acc = acc + move(outs_a[2], "tensor", dy=2).astype(F32)
    proj_a = acc[:, :W] + move(acc[:, W:].astype(BF16), "tensor", dxh=1).astype(F32)
    acc = outs_b[0].astype(F32) + move(outs_b[1], "tensor", dxh=1).astype(F32)
    proj_b = acc[:, :W]
    for dy in range(1, NY):
        proj_b = proj_b + move(
            acc[:, dy * W : dy * W + W].astype(BF16), "tensor", dy=dy
        ).astype(F32)
    proj = jnp.concatenate([proj_a, proj_b], axis=0)
    hidden_out = (hidden_in.astype(F32) + gate * proj).astype(BF16)
    return hidden_out, fresh


def solution(mesh):
    in_specs = (
        P("patch", "tensor"),
        P(None, "patch", "tensor"),
        P(),
        P(),
        P(None, None, "tensor"),
        P(),
        P(),
        P("tensor", None),
    )
    out_specs = (P("patch", "tensor"), P(None, "patch", "tensor"))
    return jax.shard_map(
        on_device, mesh=mesh, in_specs=in_specs, out_specs=out_specs, check_vma=False
    )
```

```python
import jax
import jax.numpy as jnp
from jax import lax
from jax.experimental import pallas as pl
from jax.experimental.pallas import tpu as pltpu
from jax.sharding import PartitionSpec as P

HEAD = 128
D = 3072
W = 384
HL = 3
TOK = 384
NZ, NY = 8, 4
Z4, FAR, GATE, ROWS_A, MB, COST, LN, EARLY, NEARH, FARH = 'own', True, False, 256, 16, 12, 64, True, True, ''
LOG2E = 1.4426950408889634
F32, BF16 = jnp.float32, jnp.bfloat16
VMEM = pl.BlockSpec(memory_space=pltpu.VMEM)
SMEM = pl.BlockSpec(memory_space=pltpu.SMEM)
ANY = pl.BlockSpec(memory_space=pl.ANY)
HBM = pl.BlockSpec(memory_space=pltpu.HBM)


def move(x, axis, dz=0, dxl=0, dc=0, dy=0, dxh=0):
    if axis == "patch":
        pairs = [
            (i, ((i // 4 + dz) % NZ) * 4 + (((i // 2) % 2) ^ dxl) * 2 + ((i % 2) ^ dc))
            for i in range(32)
        ]
    else:
        pairs = [(i, ((i // 2 + dy) % NY) * 2 + ((i % 2) ^ dxh)) for i in range(8)]
    return lax.ppermute(x, axis, pairs)


def call(kern, outs, n_in, flops, smem=(), hbm=(), late=(), scratch=(), name=None, mb=MB):
    return pl.pallas_call(
        kern,
        out_shape=tuple(jax.ShapeDtypeStruct(s, t) for s, t in outs),
        in_specs=[
            SMEM if i in smem else HBM if i in hbm else ANY if i in late else VMEM
            for i in range(n_in)
        ],
        out_specs=tuple(VMEM for _ in outs),
        scratch_shapes=list(scratch),
        compiler_params=pltpu.CompilerParams(vmem_limit_bytes=mb * 2**20),
        cost_estimate=pl.CostEstimate(flops=flops, bytes_accessed=4 * 2**20, transcendentals=0),
        name=name,
    )


def qkv_kernel(g_hbm, mod_ref, gain_ref, w_hbm, q_ref, f_ref, n_ref, w_ref, g_ref, sem):
    gather = pltpu.make_async_copy(g_hbm, g_ref, sem.at[3])
    gather.start()
    copies = [
        pltpu.make_async_copy(w_hbm.at[j], w_ref.at[:, j * W : j * W + W], sem.at[j])
        for j in range(3)
    ]
    for cp in copies:
        cp.start()
    n = D // W
    gather.wait()

    @pl.loop(0, TOK // LN)
    def _(r):
        rows = pl.ds(pl.multiple_of(r * LN, LN), LN)
        x = [g_ref[j, rows, :].astype(F32) for j in range(n)]
        total = x[0]
        for j in range(1, n):
            total = total + x[j]
        mean = jnp.sum(total, axis=1, keepdims=True) * (1.0 / D)
        x = [v - mean for v in x]
        total = x[0] * x[0]
        for j in range(1, n):
            total = total + x[j] * x[j]
        rstd = lax.rsqrt(jnp.sum(total, axis=1, keepdims=True) * (1.0 / D) + 1e-06)
        for j in range(n):
            cols = slice(j * W, j * W + W)
            n_ref[rows, cols] = (
                x[j] * rstd * (1.0 + mod_ref[1:2, cols]) + mod_ref[0:1, cols]
            ).astype(BF16)

    def head_norm(u, gain):
        out = []
        for h in range(HL):
            v = u[:, h * HEAD : h * HEAD + HEAD]
            ms = jnp.mean(v * v, axis=1, keepdims=True)
            out.append(v * lax.rsqrt(ms + 1e-06) * gain)
        return jnp.concatenate(out, axis=1)

    for cp in copies:
        cp.wait()
    qkv = jnp.dot(n_ref[...], w_ref[...], preferred_element_type=F32)
    q_ref[...] = head_norm(qkv[:, :W], gain_ref[0:1, :] * (HEAD**-0.5 * LOG2E)).astype(BF16)
    f_ref[0] = head_norm(qkv[:, W : 2 * W], gain_ref[1:2, :]).astype(BF16)
    f_ref[1] = qkv[:, 2 * W :].astype(BF16)


def flash(hs, q, blocks, m, l, acc):
    groups = [blocks[i : i + 2] for i in range(0, len(blocks), 2)]

    def scores(g):
        k = [kb(hs) for kb, _ in g]
        k = k[0] if len(k) == 1 else jnp.concatenate(k, axis=0)
        return lax.dot_general(q, k, (((1,), (1,)), ((), ())), preferred_element_type=F32)

    s = scores(groups[0])
    for i, g in enumerate(groups):
        nxt = scores(groups[i + 1]) if i + 1 < len(groups) else None
        top = jnp.max(s, axis=1, keepdims=True)
        new = top if m is None else jnp.maximum(m, top)
        p = jnp.exp2(s - new)
        ls = p[:, :HEAD]
        for j in range(1, p.shape[1] // HEAD):
            ls = ls + p[:, j * HEAD : j * HEAD + HEAD]
        ls = jnp.sum(ls, axis=1, keepdims=True)
        v = [vb(hs) for _, vb in g]
        v = v[0] if len(v) == 1 else jnp.concatenate(v, axis=0)
        pv = jnp.dot(p.astype(BF16), v, preferred_element_type=F32)
        if m is None:
            l, acc = ls, pv
        else:
            a = jnp.exp2(m - new)
            l, acc = l * a + ls, acc * a + pv
        m, s = new, nxt
    return m, l, acc


def views(refs, kinds):
    out, i = [], 0
    for kind in kinds:
        if kind == 2:
            r = refs[i]
            out.append((lambda hs, r=r: r[0, :, hs], lambda hs, r=r: r[1, :, hs]))
            i += 1
        else:
            rk, rv = refs[i], refs[i + 1]
            out.append((lambda hs, r=rk: r[:, hs], lambda hs, r=rv: r[:, hs]))
            i += 2
    return out


def head_slice(h):
    if isinstance(h, int):
        return pl.ds(h * HEAD, HEAD)
    return pl.ds(pl.multiple_of(h * HEAD, HEAD), HEAD)


if NEARH:
    def first_stage(q, blocks, name, after=()):
        rows = q.shape[0]
        n = len(blocks)

        def kern(q_ref, *refs):
            acc_ref, ml_ref, kv_ref, sem = refs[-4:]
            copies = [pltpu.make_async_copy(refs[i], kv_ref.at[i], sem.at[i]) for i in range(n)]
            for cp in copies:
                cp.start()
            lane = lax.broadcasted_iota(jnp.int32, (rows, HEAD), 1)
            ml_ref[...] = jnp.zeros((rows, HEAD), F32)

            def one(h, first):
                def keys(i):
                    def read(hs):
                        if first:
                            copies[i].wait()
                        return kv_ref[i, 0, :, hs]

                    return read

                kv = [(keys(i), lambda hs, i=i: kv_ref[i, 1, :, hs]) for i in range(n)]
                hs = head_slice(h)
                m, l, acc = flash(hs, q_ref[:, hs], kv, None, None, None)
                acc_ref[:, hs] = acc
                ml = jnp.where(lane == h, m, ml_ref[...])
                ml_ref[...] = jnp.where(lane == HL + h, l, ml)

            one(0, True)
            pl.loop(1, HL)(lambda h: one(h, False))

        k = 1 + n + len(after)
        return call(
            kern,
            [((rows, W), F32), ((rows, HEAD), F32)],
            k,
            COST * rows * W * TOK * n,
            hbm=range(1, 1 + n),
            late=range(1 + n, k),
            scratch=[pltpu.VMEM((n, 2, TOK, W), BF16), pltpu.SemaphoreType.DMA((n,))],
            name=name,
        )(q, *[pltpu.with_memory_space_constraint(x, pltpu.HBM) for x in blocks], *after)
else:
    def first_stage(q, blocks, name, after=()):
        rows = q.shape[0]
        kinds = [2] * len(blocks)

        def kern(q_ref, *refs):
            kv = views(refs, kinds)
            acc_ref, ml_ref = refs[-2:]
            lane = lax.broadcasted_iota(jnp.int32, (rows, HEAD), 1)
            ml_ref[...] = jnp.zeros((rows, HEAD), F32)

            @pl.loop(0, HL)
            def _(h):
                hs = head_slice(h)
                m, l, acc = flash(hs, q_ref[:, hs], kv, None, None, None)
                acc_ref[:, hs] = acc
                ml = jnp.where(lane == h, m, ml_ref[...])
                ml_ref[...] = jnp.where(lane == HL + h, l, ml)

        n = 1 + len(blocks)
        return call(
            kern,
            [((rows, W), F32), ((rows, HEAD), F32)],
            n + len(after),
            COST * rows * W * TOK * len(blocks),
            late=range(n, n + len(after)),
            name=name,
        )(q, *blocks, *after)


if FARH == 'h':
    def second_stage(q, state, refs_in, kinds, first, rows, name, after=(), cost=COST):
        n = len(refs_in)

        def kern(q_ref, acc_ref, ml_ref, *refs):
            held = refs[-1 - n : -1]
            sem = refs[-1]
            o_ref = refs[-2 - n]
            copies = [pltpu.make_async_copy(refs[i], held[i], sem.at[i]) for i in range(n)]
            for cp in copies:
                cp.start()
            rs = slice(first, first + rows)
            lane = lax.broadcasted_iota(jnp.int32, (rows, HEAD), 1)
            o_ref[:, W : W + HEAD] = jnp.zeros((rows, HEAD), BF16)

            def one(h, fetch):
                def reader(i, part, wait):
                    def read(hs):
                        if fetch and wait:
                            copies[i].wait()
                        return held[i][:, hs] if part is None else held[i][part, :, hs]

                    return read

                kv, i = [], 0
                for kind in kinds:
                    if kind == 2:
                        kv.append((reader(i, 0, True), reader(i, 1, False)))
                        i += 1
                    else:
                        kv.append((reader(i, None, True), reader(i + 1, None, True)))
                        i += 2
                hs = head_slice(h)
                ml = ml_ref[rs, :]
                m = jnp.sum(jnp.where(lane == h, ml, 0.0), axis=1, keepdims=True)
                l = jnp.sum(jnp.where(lane == HL + h, ml, 0.0), axis=1, keepdims=True)
                m, l, acc = flash(hs, q_ref[rs, hs], kv, m, l, acc_ref[rs, hs])
                o_ref[:, hs] = (acc / l).astype(BF16)
                lse = m + jnp.log2(l)
                hi = lse.astype(BF16).astype(F32)
                mid = (lse - hi).astype(BF16).astype(F32)
                low = lse - hi - mid
                row = jnp.where(lane == 3 * h, hi, 0.0)
                row = jnp.where(lane == 3 * h + 1, mid, row)
                row = jnp.where(lane == 3 * h + 2, low, row)
                o_ref[:, W : W + HEAD] = (o_ref[:, W : W + HEAD].astype(F32) + row).astype(BF16)

            one(0, True)
            pl.loop(1, HL)(lambda h: one(h, False))

        k = 3 + n + len(after)
        return call(
            kern,
            [((rows, W + HEAD), BF16)],
            k,
            cost * rows * W * TOK * len(kinds),
            hbm=range(3, 3 + n),
            late=range(3 + n, k),
            scratch=[*(pltpu.VMEM(x.shape, BF16) for x in refs_in), pltpu.SemaphoreType.DMA((n,))],
            name=name,
        )(
            q,
            *state,
            *[pltpu.with_memory_space_constraint(x, pltpu.HBM) for x in refs_in],
            *after,
        )[0]
else:
    def second_stage(q, state, refs_in, kinds, first, rows, name, after=(), cost=COST):
        def kern(q_ref, acc_ref, ml_ref, *refs):
            kv = views(refs, kinds)
            o_ref = refs[-1]
            rs = slice(first, first + rows)
            lane = lax.broadcasted_iota(jnp.int32, (rows, HEAD), 1)
            o_ref[:, W : W + HEAD] = jnp.zeros((rows, HEAD), BF16)

            @pl.loop(0, HL)
            def _(h):
                hs = head_slice(h)
                ml = ml_ref[rs, :]
                m = jnp.sum(jnp.where(lane == h, ml, 0.0), axis=1, keepdims=True)
                l = jnp.sum(jnp.where(lane == HL + h, ml, 0.0), axis=1, keepdims=True)
                m, l, acc = flash(hs, q_ref[rs, hs], kv, m, l, acc_ref[rs, hs])
                o_ref[:, hs] = (acc / l).astype(BF16)
                lse = m + jnp.log2(l)
                hi = lse.astype(BF16).astype(F32)
                mid = (lse - hi).astype(BF16).astype(F32)
                low = lse - hi - mid
                row = jnp.where(lane == 3 * h, hi, 0.0)
                row = jnp.where(lane == 3 * h + 1, mid, row)
                row = jnp.where(lane == 3 * h + 2, low, row)
                o_ref[:, W : W + HEAD] = (o_ref[:, W : W + HEAD].astype(F32) + row).astype(BF16)

        n = 3 + len(refs_in)
        return call(
            kern,
            [((rows, W + HEAD), BF16)],
            n + len(after),
            cost * rows * W * TOK * len(kinds),
            late=range(n, n + len(after)),
            name=name,
        )(q, *state, *([pltpu.with_memory_space_constraint(x, pltpu.VMEM) for x in refs_in] if FARH == 'v' else refs_in), *after)[0]


def project(mine, other, w, rank, rows, name, after=()):
    def kern(rank_ref, a_ref, b_ref, w_ref, *o_refs):
        la = a_ref[:, W : W + HEAD].astype(F32)
        lb = b_ref[:, W : W + HEAD].astype(F32)
        out = []
        for h in range(HL):
            x = jnp.sum(la[:, 3 * h : 3 * h + 3], axis=1, keepdims=True)
            y = jnp.sum(lb[:, 3 * h : 3 * h + 3], axis=1, keepdims=True)
            top = jnp.maximum(x, y)
            x, y = jnp.exp2(x - top), jnp.exp2(y - top)
            inv = 1.0 / (x + y)
            s = slice(h * HEAD, h * HEAD + HEAD)
            out.append(
                a_ref[:, s].astype(F32) * (x * inv) + b_ref[:, s].astype(F32) * (y * inv)
            )
        attn = jnp.concatenate(out, axis=1).astype(BF16)
        for j in range(8):
            cols = pl.ds(pl.multiple_of(rank_ref[j] * W, W), W)
            o_refs[j][...] = jnp.dot(
                attn, w_ref[:, cols], preferred_element_type=F32
            ).astype(BF16)

    def whole(rank_ref, a_ref, b_ref, w_ref, *o_refs):
        o_refs = o_refs[len(after) :]
        parts = []
        for o in o_refs:
            for j in range(o.shape[1] // W):
                parts.append(o.at[:, j * W : j * W + W])
        refs = [None] * 8
        for i, r in zip(layout, parts):
            refs[i] = r
        kern(rank_ref, a_ref, b_ref, w_ref, *refs)

    if name.endswith("a"):
        layout = [dy * 2 + dx for dy in range(NY) for dx in range(2)]
        outs = [((rows, 2 * W), BF16)] * 4
    else:
        layout = [dy * 2 + dx for dx in range(2) for dy in range(NY)]
        outs = [((rows, 4 * W), BF16)] * 2
    n = 4 + len(after)
    return call(
        whole, outs, n, 2 * rows * W * D, smem=(0,), late=range(4, n), name=name
    )(rank, mine, other, w, *after)


def on_device(hidden_in, stale_kv, mod_table, step_index, qkv_weight, q_gain, k_gain, out_weight):
    t_idx = lax.axis_index("tensor")
    y_idx, x_idx = t_idx // 2, t_idx % 2
    rank = jnp.stack(
        [((y_idx + dy) % NY) * 2 + (x_idx ^ dx) for dy in range(NY) for dx in range(2)]
    ).astype(jnp.int32)
    modulation = lax.dynamic_index_in_dim(mod_table, step_index[0], 0, keepdims=False)
    gate = lax.dynamic_slice_in_dim(modulation[2], t_idx * W, W, 0)
    gains = jnp.stack([q_gain, k_gain])
    in_hbm = pltpu.with_memory_space_constraint
    weight = in_hbm(jnp.transpose(qkv_weight, (1, 0, 2)), pltpu.HBM)
    tie = lax.optimization_barrier

    hidden = lax.all_to_all(
        jnp.broadcast_to(hidden_in[None], (8, TOK, W)), "tensor", 0, 0, tiled=True
    )

    def step(u, d):
        return move(u, "patch", dz=1), move(d, "patch", dz=-1)

    def swap(*xs):
        return [move(x, "patch", dc=1) for x in xs]

    x0 = stale_kv
    up1, down1 = step(x0, x0)
    up2, down2 = step(up1, down1)
    x0c, up1c, down1c = swap(x0, up1, down1)
    if EARLY:
        x0c, up1c, down1c, up2, down2 = tie((x0c, up1c, down1c, up2, down2))
    up3, down3 = step(up2, down2)
    up2c, down2c = swap(up2, down2)
    near = [x0, up1, down1, up2, down2]
    near_c = [x0c, up1c, down1c, up2c, down2c]

    q, fresh = call(
        qkv_kernel,
        [((TOK, W), BF16), ((2, TOK, W), BF16)],
        4,
        6 * TOK * D * 3 * W,
        hbm=(0, 3),
        scratch=[
            pltpu.VMEM((TOK, D), BF16),
            pltpu.VMEM((D, 3 * W), BF16),
            pltpu.VMEM((8, TOK, W), BF16),
            pltpu.SemaphoreType.DMA((4,)),
        ],
        name="qkv",
    )(in_hbm(hidden, pltpu.HBM), modulation, gains, weight)
    if Z4 == "q":
        up3, down3, q = tie((up3, down3, q))
    q_other = move(q, "patch", dxl=1)
    own1 = first_stage(q, [*near[1:], *near_c], "own_first")
    if Z4 == "own":
        up3, down3, top, q_other = tie((up3, down3, own1[1], q_other))
        own1 = [own1[0], top]
    if Z4 == "qo":
        up3, down3, q_other = tie((up3, down3, q_other))
    k4, v4 = step(up3[0], down3[1])
    par1 = first_stage(q_other, [*near, *near_c], "partner_first", after=own1[:1])
    if FAR:
        k4, v4, top = tie((k4, v4, par1[1]))
        par1 = [par1[0], top]
    far = [up3, down3, k4, v4]
    rest = [*far, *swap(*far)]
    kinds = [2, 2, 1] * 2
    rows_a, rows_b = ROWS_A, TOK - ROWS_A
    fresh_rest, fresh_kinds = [fresh, *rest], [2, *kinds]
    sent_a = second_stage(q_other, par1, rest, kinds, 0, rows_a, "partner_second_a")
    got_a = move(sent_a, "patch", dxl=1)
    mine_a = second_stage(
        q, own1, fresh_rest, fresh_kinds, 0, rows_a, "own_second_a", after=[sent_a]
    )
    outs_a = project(mine_a, got_a, out_weight, rank, rows_a, "project_a")
    near_a = [move(outs_a[dy], "tensor", dy=dy) for dy in (1, 3)]
    sent_b = second_stage(
        q_other, par1, rest, kinds, rows_a, rows_b, "partner_second_b", after=outs_a[:1]
    )
    got_b = move(sent_b, "patch", dxl=1)
    mine_b = second_stage(
        q, own1, fresh_rest, fresh_kinds, rows_a, rows_b, "own_second_b", after=[sent_b]
    )
    outs_b = project(mine_b, got_b, out_weight, rank, rows_b, "project_b", after=near_a if GATE else ())
    acc = outs_a[0].astype(F32) + near_a[0].astype(F32) + near_a[1].astype(F32)
    acc = acc + move(outs_a[2], "tensor", dy=2).astype(F32)
    proj_a = acc[:, :W] + move(acc[:, W:].astype(BF16), "tensor", dxh=1).astype(F32)
    acc = outs_b[0].astype(F32) + move(outs_b[1], "tensor", dxh=1).astype(F32)
    proj_b = acc[:, :W]
    for dy in range(1, NY):
        proj_b = proj_b + move(
            acc[:, dy * W : dy * W + W].astype(BF16), "tensor", dy=dy
        ).astype(F32)
    proj = jnp.concatenate([proj_a, proj_b], axis=0)
    hidden_out = (hidden_in.astype(F32) + gate * proj).astype(BF16)
    return hidden_out, fresh


def solution(mesh):
    in_specs = (
        P("patch", "tensor"),
        P(None, "patch", "tensor"),
        P(),
        P(),
        P(None, None, "tensor"),
        P(),
        P(),
        P("tensor", None),
    )
    out_specs = (P("patch", "tensor"), P(None, "patch", "tensor"))
    return jax.shard_map(
        on_device, mesh=mesh, in_specs=in_specs, out_specs=out_specs, check_vma=False
    )
```
